32 devices in a mesh: row: 4 (over y, x), col: 8 (over z, core).
Axes of the slice: x: 2, y: 2, z: 4, core: 2. Of those that a mesh axis runs over, the one named last changes fastest.
Arguments:
- embeddings: bfloat16 [128, 256, 256], P('col'), may hold values from -0.375 to 0.375
- projection: bfloat16 [256, 64], replicated, may hold values from -4.1875 to 4.1875
- weight: bfloat16 [16384, 32768], P('row', 'col'), may hold values from -0.046875 to 0.046875
- act_grad: bfloat16 [128, 32768], P('row', 'col'), may hold values from -6 to 6
Outputs:
- activation: bfloat16 [128, 32768], P('row', 'col')
- weight_grad: float32 [16384, 32768], P('row', 'col')
- feature_grad: float32 [128, 16384], P('col', 'row')
The draws below stay inside these ranges and needn't reach their ends.
All inputs are finite; a program needn't handle non-finite values.
Results may differ from the reference program's by a relative error of at most 0.0066.
Values may be sent and summed in bfloat16 or wider, within the bound.
A program may use at most 192 MiB of HBM per device.

```python
import jax
import jax.numpy as jnp
from jax import lax

N_EMB = 256
D_EMB = 256
PROJ = 64
H = 32768
B = 128
K = 16384


def level_of(key, shape, cuts, low, high):
    def one(dim, parts):
        heights = jax.random.uniform(jax.random.fold_in(jax.random.fold_in(key, 6), dim), (parts,), jnp.float32, low / len(cuts), high / len(cuts))
        return jnp.repeat(jnp.exp(heights), shape[dim] // parts).reshape((-1,) + (1,) * (len(shape) - dim - 1))

    factor_of = one(*cuts[0])
    for cut in cuts[1:]:
        factor_of = factor_of * one(*cut)
    return factor_of


def noise(stream_key, dims, width, bound, shards=(), kind=jnp.bfloat16):
    drawn = jax.random.normal(stream_key, dims, jnp.float32) * width
    if len(shards) > 0:
        drawn = level_of(stream_key, dims, shards, -0.22, 0.18) * drawn
    return jnp.clip(drawn, min=-bound, max=bound).astype(kind)


def setup_inputs(seed: int = 0) -> dict:
    seeds = jax.random.split(jax.random.key(seed), 5)
    return {
        "embeddings": noise(seeds[0], (B, N_EMB, D_EMB), D_EMB ** -0.5, 0.375, ((0, 8),)),
        "projection": noise(seeds[1], (N_EMB, PROJ), 0.7, 4.1875),
        "weight": noise(seeds[2], (K, H), K ** -0.5, 0.046875, ((0, 4), (1, 8))),
        "act_grad": noise(seeds[3], (B, H), 1.0, 6.0, ((0, 4), (1, 8))),
    }


def silu_slope(values):
    sig = jax.nn.sigmoid(values)
    return sig * (1.0 + values * (1.0 - sig))


def reference(embeddings, projection, weight, act_grad):
    emb_wide = embeddings.astype(jnp.float32)
    gram = jnp.einsum('bid,bmd->bim', emb_wide, emb_wide).astype(jnp.bfloat16)
    features = jnp.einsum('bim,mr->bir', gram.astype(jnp.float32), projection.astype(jnp.float32))
    features = features.astype(jnp.bfloat16).reshape(embeddings.shape[0], -1)
    preact = jnp.dot(features, weight, preferred_element_type=jnp.float32)
    activation = jax.nn.silu(preact).astype(jnp.bfloat16)
    slope_grad = (act_grad.astype(jnp.float32) * silu_slope(preact)).astype(jnp.bfloat16)
    weight_grad = lax.dot_general(features, slope_grad, (((0,), (0,)), ((), ())), preferred_element_type=jnp.float32)
    feature_grad = lax.dot_general(slope_grad, weight, (((1,), (1,)), ((), ())), preferred_element_type=jnp.float32)
    return activation, weight_grad, feature_grad
```

```python
import functools

import jax
import jax.numpy as jnp
from jax import lax
from jax.experimental import pallas as pl
from jax.experimental.pallas import tpu as pltpu
from jax.sharding import PartitionSpec as P

MESH = pl.DeviceIdType.MESH
F32 = jnp.float32
BF16 = jnp.bfloat16


def silu_slope(values, sig):
    return sig * (1.0 + values * (1.0 - sig))


def rows_at(index, size):
    return pl.ds(pl.multiple_of(index * size, size), size)


def exchange_kernel(
    n_row,
    n_col,
    chunk,
    group,
    depth_tile,
    feat_ref,
    weight_ref,
    grad_ref,
    *refs,
):
    n_chip = n_col // 2
    act_out, feat_out, slope_out, own_out = refs[:4]
    part_outs = refs[4 : 4 + n_chip - 1]
    (
        weight,
        feats,
        slopes,
        partial,
        partial_send,
        partial_recv,
        act,
        fgrad,
        sib_send,
        sib_recv,
        own,
        parts,
        weight_sem,
        out_sem,
        part_sem,
        gather_send,
        gather_recv,
        forward_send,
        forward_recv,
        reduce_send,
        reduce_recv,
        slope_send,
        slope_recv,
        sib_send_sem,
        sib_recv_sem,
    ) = refs[4 + n_chip - 1 :]

    me_row = lax.axis_index("row")
    me_col = lax.axis_index("col")
    core = lax.rem(me_col, 2)
    chip = lax.div(me_col, 2)
    sibling = chip * 2 + (1 - core)
    mine = feat_ref.shape[0]
    kept = grad_ref.shape[0]
    depth, width = weight_ref.shape
    n_chunks = width // chunk

    def chip_at(step):
        return lax.rem(chip + step, n_chip)

    def chip_back(step):
        return lax.rem(chip + n_chip - step, n_chip)

    def row_at(step):
        return lax.rem(me_row + step, n_row)

    def cols(j):
        return pl.ds(j * chunk, chunk)

    loads = []
    for j in range(n_chunks):
        load = pltpu.make_async_copy(
            weight_ref.at[:, cols(j)], weight.at[:, cols(j)], weight_sem.at[j]
        )
        load.start()
        loads.append(load)

    barrier = pltpu.get_barrier_semaphore()
    for step in range(1, n_chip):
        pl.semaphore_signal(
            barrier, inc=1, device_id=(me_row, chip_at(step) * 2 + core), device_id_type=MESH
        )
    pl.semaphore_signal(barrier, inc=1, device_id=(me_row, sibling), device_id_type=MESH)
    for step in range(1, n_row):
        pl.semaphore_signal(barrier, inc=1, device_id=(row_at(step), me_col), device_id_type=MESH)
    pl.semaphore_wait(barrier, n_chip + n_row - 1)

    sends = []
    gathers = []
    for step in range(1, n_chip):
        copy = pltpu.make_async_remote_copy(
            src_ref=feat_ref,
            dst_ref=feats.at[rows_at(me_col, mine)],
            send_sem=gather_send.at[step],
            recv_sem=gather_recv.at[step],
            device_id=(me_row, chip_at(step) * 2 + core),
            device_id_type=MESH,
        )
        copy.start()
        gathers.append(copy)
        sends.append(copy)
    forwards = []
    for step in range(n_chip):
        block = rows_at(chip_back(step) * 2 + core, mine)
        if step > 0:
            gathers[step - 1].wait_recv()
        copy = pltpu.make_async_remote_copy(
            src_ref=feat_ref if step == 0 else feats.at[block],
            dst_ref=feats.at[block],
            send_sem=forward_send.at[step],
            recv_sem=forward_recv.at[step],
            device_id=(me_row, sibling),
            device_id_type=MESH,
        )
        copy.start()
        forwards.append(copy)
        sends.append(copy)
        if step == 0:
            feats[rows_at(me_col, mine), :] = feat_ref[...]
    for copy in forwards:
        copy.wait_recv()
    outs = [pltpu.make_async_copy(feats, feat_out, out_sem.at[0])]
    outs[0].start()

    reduces = {}
    spreads = {}

    def multiply(j):
        loads[j].wait()

        @pl.loop(0, chunk // 256)
        def _(t):
            at = pl.ds(pl.multiple_of(j * chunk + t * 256, 256), 256)
            total = jnp.dot(feats[...], weight[:, at], preferred_element_type=F32)
            partial[:, at] = total
            partial_send[:, at] = total.astype(BF16)

        reduces[j] = []
        for step in range(1, n_row):
            copy = pltpu.make_async_remote_copy(
                src_ref=partial_send.at[rows_at(row_at(step), kept), cols(j)],
                dst_ref=partial_recv.at[step - 1, :, cols(j)],
                send_sem=reduce_send.at[step - 1, j],
                recv_sem=reduce_recv.at[step - 1, j],
                device_id=(row_at(step), me_col),
                device_id_type=MESH,
            )
            copy.start()
            reduces[j].append(copy)
            sends.append(copy)

    def activate(j):
        for copy in reduces[j]:
            copy.wait_recv()
        preact = partial[rows_at(me_row, kept), cols(j)]
        for step in range(1, n_row):
            preact = preact + partial_recv[step - 1, :, cols(j)].astype(F32)
        sig = 1.0 / (1.0 + jnp.exp(-preact))
        slope = grad_ref[:, cols(j)].astype(F32) * silu_slope(preact, sig)
        slopes[rows_at(me_row, kept), cols(j)] = slope.astype(BF16)
        spreads[j] = []
        for step in range(1, n_row):
            block = slopes.at[rows_at(me_row, kept), cols(j)]
            copy = pltpu.make_async_remote_copy(
                src_ref=block,
                dst_ref=block,
                send_sem=slope_send.at[step - 1, j],
                recv_sem=slope_recv.at[step - 1, j],
                device_id=(row_at(step), me_col),
                device_id_type=MESH,
            )
            copy.start()
            spreads[j].append(copy)
            sends.append(copy)
        act[:, cols(j)] = (preact * sig).astype(BF16)

    def back(g):
        for j in range(g * group, (g + 1) * group):
            for copy in spreads[j]:
                copy.wait_recv()
        units = pl.ds(g * group * chunk, group * chunk)

        @pl.loop(0, depth // depth_tile)
        def _(t):
            at = pl.ds(pl.multiple_of(t * depth_tile, depth_tile), depth_tile)
            term = lax.dot_general(
                slopes[:, units],
                weight[at, units],
                (((1,), (1,)), ((), ())),
                preferred_element_type=F32,
            )
            if g == 0:
                fgrad[:, at] = term
            else:
                fgrad[:, at] += term

    for j in range(n_chunks):
        multiply(j)
        if j >= 2:
            activate(j - 2)
    if n_chunks > 1:
        activate(n_chunks - 2)
    n_groups = n_chunks // group
    if n_groups > 1:
        back(0)
    activate(n_chunks - 1)
    outs.append(pltpu.make_async_copy(act, act_out, out_sem.at[1]))
    outs[-1].start()
    for g in range(min(1, n_groups - 1), n_groups):
        back(g)
    outs.append(pltpu.make_async_copy(slopes, slope_out, out_sem.at[2]))
    outs[-1].start()

    swaps = []
    for step in range(n_chip):
        theirs = chip_at(step) * 2 + (1 - core)
        sib_send[step] = fgrad[rows_at(theirs, mine), :].astype(BF16)
        copy = pltpu.make_async_remote_copy(
            src_ref=sib_send.at[step],
            dst_ref=sib_recv.at[step],
            send_sem=sib_send_sem.at[step],
            recv_sem=sib_recv_sem.at[step],
            device_id=(me_row, sibling),
            device_id_type=MESH,
        )
        copy.start()
        swaps.append(copy)
        sends.append(copy)
    for step in range(n_chip):
        swaps[step].wait_recv()
        total = fgrad[rows_at(chip_at(step) * 2 + core, mine), :] + sib_recv[step].astype(F32)
        if step == 0:
            own[...] = total
            outs.append(pltpu.make_async_copy(own, own_out, out_sem.at[3]))
        else:
            parts[step - 1] = total.astype(BF16)
            outs.append(
                pltpu.make_async_copy(
                    parts.at[step - 1], part_outs[step - 1], part_sem.at[step - 1]
                )
            )
        outs[-1].start()
    for copy in sends:
        copy.wait_send()
    for copy in outs:
        copy.wait()


def exchange(mesh, features, weight, act_grad):
    n_row, n_col = mesh.shape["row"], mesh.shape["col"]
    n_chip = n_col // 2
    mine, depth = features.shape
    kept, width = act_grad.shape
    examples = mine * n_col
    chunk = width // 8 if width >= 4096 else width
    n_chunks = width // chunk
    group = min(2, n_chunks)
    depth_tile = min(512, depth)
    anywhere = pl.BlockSpec(memory_space=pl.ANY)
    vmem = pl.BlockSpec(memory_space=pltpu.VMEM)
    flops = 4 * examples * depth * width
    dma = pltpu.SemaphoreType.DMA
    return pl.pallas_call(
        functools.partial(exchange_kernel, n_row, n_col, chunk, group, depth_tile),
        out_shape=[
            jax.ShapeDtypeStruct((kept, width), BF16),
            jax.ShapeDtypeStruct((examples, depth), BF16),
            jax.ShapeDtypeStruct((examples, width), BF16),
            jax.ShapeDtypeStruct((mine, depth), F32),
        ]
        + [jax.ShapeDtypeStruct((mine, depth), BF16)] * (n_chip - 1),
        in_specs=[vmem, anywhere, vmem],
        out_specs=[anywhere] * (4 + n_chip - 1),
        scratch_shapes=[
            pltpu.VMEM((depth, width), BF16),
            pltpu.VMEM((examples, depth), BF16),
            pltpu.VMEM((examples, width), BF16),
            pltpu.VMEM((examples, width), F32),
            pltpu.VMEM((examples, width), BF16),
            pltpu.VMEM((n_row - 1, kept, width), BF16),
            pltpu.VMEM((kept, width), BF16),
            pltpu.VMEM((examples, depth), F32),
            pltpu.VMEM((n_chip, mine, depth), BF16),
            pltpu.VMEM((n_chip, mine, depth), BF16),
            pltpu.VMEM((mine, depth), F32),
            pltpu.VMEM((n_chip - 1, mine, depth), BF16),
            dma((n_chunks,)),
            dma((4,)),
            dma((n_chip - 1,)),
            dma((n_chip,)),
            dma((n_chip,)),
            dma((n_chip,)),
            dma((n_chip,)),
            dma((n_row - 1, n_chunks)),
            dma((n_row - 1, n_chunks)),
            dma((n_row - 1, n_chunks)),
            dma((n_row - 1, n_chunks)),
            dma((n_chip,)),
            dma((n_chip,)),
        ],
        compiler_params=pltpu.CompilerParams(
            collective_id=0, has_side_effects=True, vmem_limit_bytes=56 * 1024 * 1024
        ),
        cost_estimate=pl.CostEstimate(
            flops=flops, bytes_accessed=2 * depth * width, transcendentals=kept * width
        ),
    )(features, weight, act_grad)


def outer_kernel(feat_ref, slope_ref, out_ref):
    out_ref[...] = lax.dot_general(
        feat_ref[...], slope_ref[...], (((0,), (0,)), ((), ())), preferred_element_type=F32
    )


def outer(features, slopes):
    examples, depth = features.shape
    width = slopes.shape[1]
    tile = min(256, depth)
    return pl.pallas_call(
        outer_kernel,
        grid=(depth // tile,),
        out_shape=jax.ShapeDtypeStruct((depth, width), F32),
        in_specs=[
            pl.BlockSpec((examples, tile), lambda i: (0, i)),
            pl.BlockSpec((examples, width), lambda i: (0, 0)),
        ],
        out_specs=pl.BlockSpec((tile, width), lambda i: (i, 0)),
        compiler_params=pltpu.CompilerParams(vmem_limit_bytes=32 * 1024 * 1024),
        cost_estimate=pl.CostEstimate(
            flops=2 * examples * depth * width,
            bytes_accessed=4 * depth * width,
            transcendentals=0,
        ),
    )(features, slopes)


def shards(mesh, embeddings, projection, weight, act_grad):
    n_chip = mesh.shape["col"] // 2
    emb_rows = weight.shape[0] // projection.shape[1]
    emb_first = lax.axis_index("row") * emb_rows
    mine_emb = lax.dynamic_slice_in_dim(embeddings, emb_first, emb_rows, 1)
    gram = jnp.einsum(
        "bid,bmd->bim", mine_emb, embeddings, preferred_element_type=F32
    ).astype(BF16)
    features = jnp.einsum("bim,mr->bir", gram, projection, preferred_element_type=F32)
    features = features.astype(BF16).reshape(embeddings.shape[0], -1)
    activation, features_all, slopes_all, own, *parts = exchange(
        mesh, features, weight, act_grad
    )
    arrived = []
    for step in range(1, n_chip):
        pairs = [
            (2 * z + core, 2 * ((z + step) % n_chip) + core)
            for z in range(n_chip)
            for core in range(2)
        ]
        arrived.append(lax.ppermute(parts[step - 1], "col", pairs))
    weight_grad = outer(features_all, slopes_all)
    feature_grad = own
    for block in arrived:
        feature_grad = feature_grad + block.astype(F32)
    return activation, weight_grad, feature_grad


def solution(mesh):
    return jax.shard_map(
        functools.partial(shards, mesh),
        mesh=mesh,
        in_specs=(P("col", None, None), P(), P("row", "col"), P("row", "col")),
        out_specs=(P("row", "col"), P("row", "col"), P("col", "row")),
        check_vma=False,
    )
```

```python
import functools

import jax
import jax.numpy as jnp
from jax import lax
from jax.experimental import pallas as pl
from jax.experimental.pallas import tpu as pltpu
from jax.sharding import PartitionSpec as P

MESH = pl.DeviceIdType.MESH
F32 = jnp.float32
BF16 = jnp.bfloat16


def silu_slope(values, sig):
    return sig * (1.0 + values * (1.0 - sig))


def rows_at(index, size):
    return pl.ds(pl.multiple_of(index * size, size), size)


def exchange_kernel(
    n_row,
    n_col,
    chunk,
    pieces,
    groups,
    depth_tile,
    feat_ref,
    weight_ref,
    grad_ref,
    *refs,
):
    n_chip = n_col // 2
    act_out, feat_out, slope_out, own_out = refs[:4]
    part_outs = refs[4 : 4 + n_chip - 1]
    (
        weight,
        feats,
        slopes,
        partial,
        partial_send,
        partial_recv,
        act,
        slopes_t,
        fgrad_t,
        fgrad,
        sib_send,
        sib_recv,
        own,
        parts,
        weight_sem,
        out_sem,
        part_sem,
        gather_send,
        gather_recv,
        forward_send,
        forward_recv,
        reduce_send,
        reduce_recv,
        slope_send,
        slope_recv,
        sib_send_sem,
        sib_recv_sem,
    ) = refs[4 + n_chip - 1 :]

    me_row = lax.axis_index("row")
    me_col = lax.axis_index("col")
    core = lax.rem(me_col, 2)
    chip = lax.div(me_col, 2)
    sibling = chip * 2 + (1 - core)
    mine = feat_ref.shape[0]
    kept = grad_ref.shape[0]
    depth, width = weight_ref.shape
    n_chunks = width // chunk

    def chip_at(step):
        return lax.rem(chip + step, n_chip)

    def chip_back(step):
        return lax.rem(chip + n_chip - step, n_chip)

    def row_at(step):
        return lax.rem(me_row + step, n_row)

    def cols(j):
        return pl.ds(j * chunk, chunk)

    piece = depth // pieces

    def span(p):
        return pl.ds(p * piece, piece)

    loads = []
    for p in range(pieces):
        load = pltpu.make_async_copy(
            weight_ref.at[span(p), :], weight.at[span(p), :], weight_sem.at[p]
        )
        load.start()
        loads.append(load)

    barrier = pltpu.get_barrier_semaphore()
    for step in range(1, n_chip):
        pl.semaphore_signal(
            barrier, inc=1, device_id=(me_row, chip_at(step) * 2 + core), device_id_type=MESH
        )
    pl.semaphore_signal(barrier, inc=1, device_id=(me_row, sibling), device_id_type=MESH)
    for step in range(1, n_row):
        pl.semaphore_signal(barrier, inc=1, device_id=(row_at(step), me_col), device_id_type=MESH)
    pl.semaphore_wait(barrier, n_chip + n_row - 1)

    sends = []
    gathers = {}
    for p in range(pieces):
        for step in range(1, n_chip):
            copy = pltpu.make_async_remote_copy(
                src_ref=feat_ref.at[:, span(p)],
                dst_ref=feats.at[rows_at(me_col, mine), span(p)],
                send_sem=gather_send.at[step, p],
                recv_sem=gather_recv.at[step, p],
                device_id=(me_row, chip_at(step) * 2 + core),
                device_id_type=MESH,
            )
            copy.start()
            gathers[p, step] = copy
            sends.append(copy)
    feats[rows_at(me_col, mine), :] = feat_ref[...]
    forwards = {}

    def forward(p, step):
        block = feats.at[rows_at(chip_back(step) * 2 + core, mine), span(p)]
        if step > 0:
            gathers[p, step].wait_recv()
        copy = pltpu.make_async_remote_copy(
            src_ref=feat_ref.at[:, span(p)] if step == 0 else block,
            dst_ref=block,
            send_sem=forward_send.at[step, p],
            recv_sem=forward_recv.at[step, p],
            device_id=(me_row, sibling),
            device_id_type=MESH,
        )
        copy.start()
        forwards[p, step] = copy
        sends.append(copy)

    for p in range(pieces):
        forward(p, 0)
    for step in range(1, n_chip):
        forward(0, step)

    def multiply_part(p, first, count):
        @pl.loop(0, count // 256)
        def _(t):
            at = pl.ds(pl.multiple_of(first + t * 256, 256), 256)
            term = jnp.dot(feats[:, span(p)], weight[span(p), at], preferred_element_type=F32)
            total = term if p == 0 else partial[:, at] + term
            partial[:, at] = total
            if p == pieces - 1:
                partial_send[:, at] = total.astype(BF16)

    outs = []
    for p in range(pieces):
        for step in range(n_chip):
            forwards[p, step].wait_recv()
        loads[p].wait()
        if p < pieces - 1:
            multiply_part(p, 0, width // 2)
            for step in range(1, n_chip):
                forward(p + 1, step)
            multiply_part(p, width // 2, width // 2)
    outs.append(pltpu.make_async_copy(feats, feat_out, out_sem.at[0]))
    outs[0].start()

    reduces = {}
    spreads = {}

    def multiply(j):
        multiply_part(pieces - 1, j * chunk, chunk)
        reduces[j] = []
        for step in range(1, n_row):
            copy = pltpu.make_async_remote_copy(
                src_ref=partial_send.at[rows_at(row_at(step), kept), cols(j)],
                dst_ref=partial_recv.at[step - 1, :, cols(j)],
                send_sem=reduce_send.at[step - 1, j],
                recv_sem=reduce_recv.at[step - 1, j],
                device_id=(row_at(step), me_col),
                device_id_type=MESH,
            )
            copy.start()
            reduces[j].append(copy)
            sends.append(copy)

    def activate(j):
        for copy in reduces[j]:
            copy.wait_recv()
        preact = partial[rows_at(me_row, kept), cols(j)]
        for step in range(1, n_row):
            preact = preact + partial_recv[step - 1, :, cols(j)].astype(F32)
        sig = 1.0 / (1.0 + jnp.exp(-preact))
        slope = grad_ref[:, cols(j)].astype(F32) * silu_slope(preact, sig)
        slopes[rows_at(me_row, kept), cols(j)] = slope.astype(BF16)
        spreads[j] = []
        for step in range(1, n_row):
            block = slopes.at[rows_at(me_row, kept), cols(j)]
            copy = pltpu.make_async_remote_copy(
                src_ref=block,
                dst_ref=block,
                send_sem=slope_send.at[step - 1, j],
                recv_sem=slope_recv.at[step - 1, j],
                device_id=(row_at(step), me_col),
                device_id_type=MESH,
            )
            copy.start()
            spreads[j].append(copy)
            sends.append(copy)
        act[:, cols(j)] = (preact * sig).astype(BF16)

    def arrive(g):
        first, last = groups[g]
        for j in range(first, last):
            for copy in spreads[j]:
                copy.wait_recv()
            slopes_t[cols(j), :] = slopes[:, cols(j)].T

    def back(g, part, n_parts):
        first, last = groups[g]
        units = pl.ds(first * chunk, (last - first) * chunk)
        base = part * (depth // n_parts)

        @pl.loop(0, depth // n_parts // depth_tile)
        def _(t):
            at = pl.ds(pl.multiple_of(base + t * depth_tile, depth_tile), depth_tile)
            total = jnp.dot(weight[at, units], slopes_t[units, :], preferred_element_type=F32)
            if g > 0:
                total = total + fgrad_t[at, :]
            if g < len(groups) - 1:
                fgrad_t[at, :] = total
            else:
                fgrad[:, at] = total.T

    for j in range(n_chunks):
        multiply(j)
        if j >= 2:
            activate(j - 2)
    if n_chunks > 1:
        activate(n_chunks - 2)
    if len(groups) > 1:
        arrive(0)
        back(0, 0, 2)
    activate(n_chunks - 1)
    outs.append(pltpu.make_async_copy(act, act_out, out_sem.at[1]))
    outs[-1].start()
    if len(groups) > 1:
        back(0, 1, 2)
    for g in range(1, len(groups) - 1):
        arrive(g)
        back(g, 0, 1)
    arrive(len(groups) - 1)
    outs.append(pltpu.make_async_copy(slopes, slope_out, out_sem.at[2]))
    outs[-1].start()

    swaps = []
    for p in range(pieces):
        back(len(groups) - 1, p, pieces)
        for step in range(n_chip):
            theirs = chip_at(step) * 2 + (1 - core)
            sib_send[step, :, span(p)] = fgrad[rows_at(theirs, mine), span(p)].astype(BF16)
        copy = pltpu.make_async_remote_copy(
            src_ref=sib_send.at[:, :, span(p)],
            dst_ref=sib_recv.at[:, :, span(p)],
            send_sem=sib_send_sem.at[p],
            recv_sem=sib_recv_sem.at[p],
            device_id=(me_row, sibling),
            device_id_type=MESH,
        )
        copy.start()
        swaps.append(copy)
        sends.append(copy)
    for p in range(pieces):
        swaps[p].wait_recv()
        for step in range(n_chip):
            held = fgrad[rows_at(chip_at(step) * 2 + core, mine), span(p)]
            total = held + sib_recv[step, :, span(p)].astype(F32)
            if step == 0:
                own[:, span(p)] = total
            else:
                parts[step - 1, :, span(p)] = total.astype(BF16)
    for step in range(1, n_chip):
        outs.append(
            pltpu.make_async_copy(parts.at[step - 1], part_outs[step - 1], part_sem.at[step - 1])
        )
        outs[-1].start()
    outs.append(pltpu.make_async_copy(own, own_out, out_sem.at[3]))
    outs[-1].start()
    for copy in sends:
        copy.wait_send()
    for copy in outs:
        copy.wait()


def exchange(mesh, features, weight, act_grad):
    n_row, n_col = mesh.shape["row"], mesh.shape["col"]
    n_chip = n_col // 2
    mine, depth = features.shape
    kept, width = act_grad.shape
    examples = mine * n_col
    chunk = width // 8 if width >= 4096 else width
    n_chunks = width // chunk
    pieces = 4 if depth >= 4096 else 1
    groups = ((0, 4), (4, 6), (6, 8)) if n_chunks == 8 else ((0, n_chunks),)
    depth_tile = min(512, depth)
    anywhere = pl.BlockSpec(memory_space=pl.ANY)
    vmem = pl.BlockSpec(memory_space=pltpu.VMEM)
    flops = 4 * examples * depth * width
    dma = pltpu.SemaphoreType.DMA
    return pl.pallas_call(
        functools.partial(exchange_kernel, n_row, n_col, chunk, pieces, groups, depth_tile),
        out_shape=[
            jax.ShapeDtypeStruct((kept, width), BF16),
            jax.ShapeDtypeStruct((examples, depth), BF16),
            jax.ShapeDtypeStruct((examples, width), BF16),
            jax.ShapeDtypeStruct((mine, depth), F32),
        ]
        + [jax.ShapeDtypeStruct((mine, depth), BF16)] * (n_chip - 1),
        in_specs=[vmem, anywhere, vmem],
        out_specs=[anywhere] * (4 + n_chip - 1),
        scratch_shapes=[
            pltpu.VMEM((depth, width), BF16),
            pltpu.VMEM((examples, depth), BF16),
            pltpu.VMEM((examples, width), BF16),
            pltpu.VMEM((examples, width), F32),
            pltpu.VMEM((examples, width), BF16),
            pltpu.VMEM((n_row - 1, kept, width), BF16),
            pltpu.VMEM((kept, width), BF16),
            pltpu.VMEM((width, examples), BF16),
            pltpu.VMEM((depth, examples), F32),
            pltpu.VMEM((examples, depth), F32),
            pltpu.VMEM((n_chip, mine, depth), BF16),
            pltpu.VMEM((n_chip, mine, depth), BF16),
            pltpu.VMEM((mine, depth), F32),
            pltpu.VMEM((n_chip - 1, mine, depth), BF16),
            dma((pieces,)),
            dma((4,)),
            dma((n_chip - 1,)),
            dma((n_chip, pieces)),
            dma((n_chip, pieces)),
            dma((n_chip, pieces)),
            dma((n_chip, pieces)),
            dma((n_row - 1, n_chunks)),
            dma((n_row - 1, n_chunks)),
            dma((n_row - 1, n_chunks)),
            dma((n_row - 1, n_chunks)),
            dma((pieces,)),
            dma((pieces,)),
        ],
        compiler_params=pltpu.CompilerParams(
            collective_id=0, has_side_effects=True, vmem_limit_bytes=56 * 1024 * 1024
        ),
        cost_estimate=pl.CostEstimate(
            flops=flops, bytes_accessed=2 * depth * width, transcendentals=kept * width
        ),
    )(features, weight, act_grad)


def outer_kernel(feat_ref, slope_ref, out_ref):
    out_ref[...] = lax.dot_general(
        feat_ref[...], slope_ref[...], (((0,), (0,)), ((), ())), preferred_element_type=F32
    )


def outer(features, slopes):
    examples, depth = features.shape
    width = slopes.shape[1]
    tall, wide = min(1024, depth), min(1024, width)
    return pl.pallas_call(
        outer_kernel,
        grid=(depth // tall, width // wide),
        out_shape=jax.ShapeDtypeStruct((depth, width), F32),
        in_specs=[
            pl.BlockSpec((examples, tall), lambda i, j: (0, i)),
            pl.BlockSpec((examples, wide), lambda i, j: (0, j)),
        ],
        out_specs=pl.BlockSpec((tall, wide), lambda i, j: (i, j)),
        compiler_params=pltpu.CompilerParams(vmem_limit_bytes=60 * 1024 * 1024),
        cost_estimate=pl.CostEstimate(
            flops=2 * examples * depth * width,
            bytes_accessed=4 * depth * width,
            transcendentals=0,
        ),
    )(features, slopes)


def shards(mesh, embeddings, projection, weight, act_grad):
    n_chip = mesh.shape["col"] // 2
    emb_rows = weight.shape[0] // projection.shape[1]
    emb_first = lax.axis_index("row") * emb_rows
    mine_emb = lax.dynamic_slice_in_dim(embeddings, emb_first, emb_rows, 1)
    gram = jnp.einsum(
        "bid,bmd->bim", mine_emb, embeddings, preferred_element_type=F32
    ).astype(BF16)
    features = jnp.einsum("bim,mr->bir", gram, projection, preferred_element_type=F32)
    features = features.astype(BF16).reshape(embeddings.shape[0], -1)
    activation, features_all, slopes_all, own, *parts = exchange(
        mesh, features, weight, act_grad
    )
    arrived = []
    for step in range(1, n_chip):
        pairs = [
            (2 * z + core, 2 * ((z + step) % n_chip) + core)
            for z in range(n_chip)
            for core in range(2)
        ]
        arrived.append(lax.ppermute(parts[step - 1], "col", pairs))
    weight_grad = outer(features_all, slopes_all)
    feature_grad = own
    for block in arrived:
        feature_grad = feature_grad + block.astype(F32)
    return activation, weight_grad, feature_grad


def solution(mesh):
    return jax.shard_map(
        functools.partial(shards, mesh),
        mesh=mesh,
        in_specs=(P("col", None, None), P(), P("row", "col"), P("row", "col")),
        out_specs=(P("row", "col"), P("row", "col"), P("col", "row")),
        check_vma=False,
    )
```

```python
import functools

import jax
import jax.numpy as jnp
from jax import lax
from jax.experimental import pallas as pl
from jax.experimental.pallas import tpu as pltpu
from jax.sharding import PartitionSpec as P

MESH = pl.DeviceIdType.MESH
F32 = jnp.float32
BF16 = jnp.bfloat16


def silu_slope(values, sig):
    return sig * (1.0 + values * (1.0 - sig))


def rows_at(index, size):
    return pl.ds(pl.multiple_of(index * size, size), size)


def exchange_kernel(
    n_row,
    n_col,
    chunk,
    pieces,
    groups,
    depth_tile,
    feat_ref,
    weight_ref,
    grad_ref,
    *refs,
):
    n_chip = n_col // 2
    act_out, feat_out, slope_out, own_out = refs[:4]
    part_outs = refs[4 : 4 + n_chip - 1]
    (
        weight,
        feats,
        slopes,
        partial,
        partial_send,
        partial_recv,
        act,
        slopes_t,
        fgrad_t,
        fgrad,
        sib_send,
        sib_recv,
        own,
        parts,
        weight_sem,
        out_sem,
        part_sem,
        gather_send,
        gather_recv,
        forward_send,
        forward_recv,
        reduce_send,
        reduce_recv,
        slope_send,
        slope_recv,
        sib_send_sem,
        sib_recv_sem,
    ) = refs[4 + n_chip - 1 :]

    me_row = lax.axis_index("row")
    me_col = lax.axis_index("col")
    core = lax.rem(me_col, 2)
    chip = lax.div(me_col, 2)
    sibling = chip * 2 + (1 - core)
    mine = feat_ref.shape[0]
    kept = grad_ref.shape[0]
    depth, width = weight_ref.shape
    n_chunks = width // chunk

    def chip_at(step):
        return lax.rem(chip + step, n_chip)

    def chip_back(step):
        return lax.rem(chip + n_chip - step, n_chip)

    def row_at(step):
        return lax.rem(me_row + step, n_row)

    def cols(j):
        return pl.ds(j * chunk, chunk)

    piece = depth // pieces

    def span(p):
        return pl.ds(p * piece, piece)

    loads = []
    for j in range(n_chunks):
        load = pltpu.make_async_copy(
            weight_ref.at[:, cols(j)], weight.at[:, cols(j)], weight_sem.at[j]
        )
        load.start()
        loads.append(load)

    barrier = pltpu.get_barrier_semaphore()
    for step in range(1, n_chip):
        pl.semaphore_signal(
            barrier, inc=1, device_id=(me_row, chip_at(step) * 2 + core), device_id_type=MESH
        )
    pl.semaphore_signal(barrier, inc=1, device_id=(me_row, sibling), device_id_type=MESH)
    for step in range(1, n_row):
        pl.semaphore_signal(barrier, inc=1, device_id=(row_at(step), me_col), device_id_type=MESH)
    pl.semaphore_wait(barrier, n_chip + n_row - 1)

    sends = []
    gathers = []
    for step in range(1, n_chip):
        copy = pltpu.make_async_remote_copy(
            src_ref=feat_ref,
            dst_ref=feats.at[rows_at(me_col, mine)],
            send_sem=gather_send.at[step],
            recv_sem=gather_recv.at[step],
            device_id=(me_row, chip_at(step) * 2 + core),
            device_id_type=MESH,
        )
        copy.start()
        gathers.append(copy)
        sends.append(copy)
    forwards = []
    for step in range(n_chip):
        block = rows_at(chip_back(step) * 2 + core, mine)
        if step > 0:
            gathers[step - 1].wait_recv()
        copy = pltpu.make_async_remote_copy(
            src_ref=feat_ref if step == 0 else feats.at[block],
            dst_ref=feats.at[block],
            send_sem=forward_send.at[step],
            recv_sem=forward_recv.at[step],
            device_id=(me_row, sibling),
            device_id_type=MESH,
        )
        copy.start()
        forwards.append(copy)
        sends.append(copy)
        if step == 0:
            feats[rows_at(me_col, mine), :] = feat_ref[...]
    for copy in forwards:
        copy.wait_recv()
    outs = [pltpu.make_async_copy(feats, feat_out, out_sem.at[0])]
    outs[0].start()

    reduces = {}
    spreads = {}

    def multiply(j):
        loads[j].wait()
        total = jnp.dot(feats[...], weight[:, cols(j)], preferred_element_type=F32)
        partial[:, cols(j)] = total
        partial_send[:, cols(j)] = total.astype(BF16)
        reduces[j] = []
        for step in range(1, n_row):
            copy = pltpu.make_async_remote_copy(
                src_ref=partial_send.at[rows_at(row_at(step), kept), cols(j)],
                dst_ref=partial_recv.at[step - 1, :, cols(j)],
                send_sem=reduce_send.at[step - 1, j],
                recv_sem=reduce_recv.at[step - 1, j],
                device_id=(row_at(step), me_col),
                device_id_type=MESH,
            )
            copy.start()
            reduces[j].append(copy)
            sends.append(copy)

    def activate(j):
        for copy in reduces[j]:
            copy.wait_recv()
        preact = partial[rows_at(me_row, kept), cols(j)]
        for step in range(1, n_row):
            preact = preact + partial_recv[step - 1, :, cols(j)].astype(F32)
        sig = 1.0 / (1.0 + jnp.exp(-preact))
        slope = grad_ref[:, cols(j)].astype(F32) * silu_slope(preact, sig)
        slopes[rows_at(me_row, kept), cols(j)] = slope.astype(BF16)
        spreads[j] = []
        for step in range(1, n_row):
            block = slopes.at[rows_at(me_row, kept), cols(j)]
            copy = pltpu.make_async_remote_copy(
                src_ref=block,
                dst_ref=block,
                send_sem=slope_send.at[step - 1, j],
                recv_sem=slope_recv.at[step - 1, j],
                device_id=(row_at(step), me_col),
                device_id_type=MESH,
            )
            copy.start()
            spreads[j].append(copy)
            sends.append(copy)
        act[:, cols(j)] = (preact * sig).astype(BF16)

    def arrive(g):
        first, last = groups[g]
        for j in range(first, last):
            for copy in spreads[j]:
                copy.wait_recv()
            slopes_t[cols(j), :] = slopes[:, cols(j)].T

    def back(g, part, n_parts):
        first, last = groups[g]
        units = pl.ds(first * chunk, (last - first) * chunk)
        base = part * (depth // n_parts)

        @pl.loop(0, depth // n_parts // depth_tile)
        def _(t):
            at = pl.ds(pl.multiple_of(base + t * depth_tile, depth_tile), depth_tile)
            total = jnp.dot(weight[at, units], slopes_t[units, :], preferred_element_type=F32)
            if g > 0:
                total = total + fgrad_t[at, :]
            if g < len(groups) - 1:
                fgrad_t[at, :] = total
            else:
                fgrad[:, at] = total.T

    for j in range(n_chunks):
        multiply(j)
        if j >= 2:
            activate(j - 2)
    if n_chunks > 1:
        activate(n_chunks - 2)
    if len(groups) > 1:
        arrive(0)
        back(0, 0, 2)
    activate(n_chunks - 1)
    outs.append(pltpu.make_async_copy(act, act_out, out_sem.at[1]))
    outs[-1].start()
    if len(groups) > 1:
        back(0, 1, 2)
    for g in range(1, len(groups) - 1):
        arrive(g)
        back(g, 0, 1)
    arrive(len(groups) - 1)
    outs.append(pltpu.make_async_copy(slopes, slope_out, out_sem.at[2]))
    outs[-1].start()

    swaps = []
    for p in range(pieces):
        back(len(groups) - 1, p, pieces)
        for step in range(n_chip):
            theirs = chip_at(step) * 2 + (1 - core)
            sib_send[step, :, span(p)] = fgrad[rows_at(theirs, mine), span(p)].astype(BF16)
        copy = pltpu.make_async_remote_copy(
            src_ref=sib_send.at[:, :, span(p)],
            dst_ref=sib_recv.at[:, :, span(p)],
            send_sem=sib_send_sem.at[p],
            recv_sem=sib_recv_sem.at[p],
            device_id=(me_row, sibling),
            device_id_type=MESH,
        )
        copy.start()
        swaps.append(copy)
        sends.append(copy)
    for p in range(pieces):
        swaps[p].wait_recv()
        for step in range(n_chip):
            held = fgrad[rows_at(chip_at(step) * 2 + core, mine), span(p)]
            total = held + sib_recv[step, :, span(p)].astype(F32)
            if step == 0:
                own[:, span(p)] = total
            else:
                parts[step - 1, :, span(p)] = total.astype(BF16)
    for step in range(1, n_chip):
        outs.append(
            pltpu.make_async_copy(parts.at[step - 1], part_outs[step - 1], part_sem.at[step - 1])
        )
        outs[-1].start()
    outs.append(pltpu.make_async_copy(own, own_out, out_sem.at[3]))
    outs[-1].start()
    for copy in sends:
        copy.wait_send()
    for copy in outs:
        copy.wait()


def exchange(mesh, features, weight, act_grad):
    n_row, n_col = mesh.shape["row"], mesh.shape["col"]
    n_chip = n_col // 2
    mine, depth = features.shape
    kept, width = act_grad.shape
    examples = mine * n_col
    chunk = width // 8 if width >= 4096 else width
    n_chunks = width // chunk
    pieces = 4 if depth >= 4096 else 1
    groups = ((0, 4), (4, 8)) if n_chunks == 8 else ((0, n_chunks),)
    depth_tile = min(1024, depth)
    anywhere = pl.BlockSpec(memory_space=pl.ANY)
    vmem = pl.BlockSpec(memory_space=pltpu.VMEM)
    flops = 4 * examples * depth * width
    dma = pltpu.SemaphoreType.DMA
    return pl.pallas_call(
        functools.partial(exchange_kernel, n_row, n_col, chunk, pieces, groups, depth_tile),
        out_shape=[
            jax.ShapeDtypeStruct((kept, width), BF16),
            jax.ShapeDtypeStruct((examples, depth), BF16),
            jax.ShapeDtypeStruct((examples, width), BF16),
            jax.ShapeDtypeStruct((mine, depth), F32),
        ]
        + [jax.ShapeDtypeStruct((mine, depth), BF16)] * (n_chip - 1),
        in_specs=[vmem, anywhere, vmem],
        out_specs=[anywhere] * (4 + n_chip - 1),
        scratch_shapes=[
            pltpu.VMEM((depth, width), BF16),
            pltpu.VMEM((examples, depth), BF16),
            pltpu.VMEM((examples, width), BF16),
            pltpu.VMEM((examples, width), F32),
            pltpu.VMEM((examples, width), BF16),
            pltpu.VMEM((n_row - 1, kept, width), BF16),
            pltpu.VMEM((kept, width), BF16),
            pltpu.VMEM((width, examples), BF16),
            pltpu.VMEM((depth, examples), F32),
            pltpu.VMEM((examples, depth), F32),
            pltpu.VMEM((n_chip, mine, depth), BF16),
            pltpu.VMEM((n_chip, mine, depth), BF16),
            pltpu.VMEM((mine, depth), F32),
            pltpu.VMEM((n_chip - 1, mine, depth), BF16),
            dma((n_chunks,)),
            dma((4,)),
            dma((n_chip - 1,)),
            dma((n_chip,)),
            dma((n_chip,)),
            dma((n_chip,)),
            dma((n_chip,)),
            dma((n_row - 1, n_chunks)),
            dma((n_row - 1, n_chunks)),
            dma((n_row - 1, n_chunks)),
            dma((n_row - 1, n_chunks)),
            dma((pieces,)),
            dma((pieces,)),
        ],
        compiler_params=pltpu.CompilerParams(
            collective_id=0, has_side_effects=True, vmem_limit_bytes=56 * 1024 * 1024
        ),
        cost_estimate=pl.CostEstimate(
            flops=flops, bytes_accessed=2 * depth * width, transcendentals=kept * width
        ),
    )(features, weight, act_grad)


def outer_kernel(feat_ref, slope_ref, out_ref):
    out_ref[...] = lax.dot_general(
        feat_ref[...], slope_ref[...], (((0,), (0,)), ((), ())), preferred_element_type=F32
    )


def outer(features, slopes):
    examples, depth = features.shape
    width = slopes.shape[1]
    tall, wide = min(1024, depth), min(1024, width)
    return pl.pallas_call(
        outer_kernel,
        grid=(depth // tall, width // wide),
        out_shape=jax.ShapeDtypeStruct((depth, width), F32),
        in_specs=[
            pl.BlockSpec((examples, tall), lambda i, j: (0, i)),
            pl.BlockSpec((examples, wide), lambda i, j: (0, j)),
        ],
        out_specs=pl.BlockSpec((tall, wide), lambda i, j: (i, j)),
        compiler_params=pltpu.CompilerParams(vmem_limit_bytes=60 * 1024 * 1024),
        cost_estimate=pl.CostEstimate(
            flops=2 * examples * depth * width,
            bytes_accessed=4 * depth * width,
            transcendentals=0,
        ),
    )(features, slopes)


def shards(mesh, embeddings, projection, weight, act_grad):
    n_chip = mesh.shape["col"] // 2
    emb_rows = weight.shape[0] // projection.shape[1]
    emb_first = lax.axis_index("row") * emb_rows
    mine_emb = lax.dynamic_slice_in_dim(embeddings, emb_first, emb_rows, 1)
    gram = jnp.einsum(
        "bid,bmd->bim", mine_emb, embeddings, preferred_element_type=F32
    ).astype(BF16)
    features = jnp.einsum("bim,mr->bir", gram, projection, preferred_element_type=F32)
    features = features.astype(BF16).reshape(embeddings.shape[0], -1)
    activation, features_all, slopes_all, own, *parts = exchange(
        mesh, features, weight, act_grad
    )
    arrived = []
    for step in range(1, n_chip):
        pairs = [
            (2 * z + core, 2 * ((z + step) % n_chip) + core)
            for z in range(n_chip)
            for core in range(2)
        ]
        arrived.append(lax.ppermute(parts[step - 1], "col", pairs))
    weight_grad = outer(features_all, slopes_all)
    feature_grad = own
    for block in arrived:
        feature_grad = feature_grad + block.astype(F32)
    return activation, weight_grad, feature_grad


def solution(mesh):
    return jax.shard_map(
        functools.partial(shards, mesh),
        mesh=mesh,
        in_specs=(P("col", None, None), P(), P("row", "col"), P("row", "col")),
        out_specs=(P("row", "col"), P("row", "col"), P("col", "row")),
        check_vma=False,
    )
```

```python
import functools

import jax
import jax.numpy as jnp
from jax import lax
from jax.experimental import pallas as pl
from jax.experimental.pallas import tpu as pltpu
from jax.sharding import PartitionSpec as P

MESH = pl.DeviceIdType.MESH
F32 = jnp.float32
BF16 = jnp.bfloat16


def silu_slope(values, sig):
    return sig * (1.0 + values * (1.0 - sig))


def rows_at(index, size):
    return pl.ds(pl.multiple_of(index * size, size), size)


def exchange_kernel(
    n_row,
    n_col,
    chunk,
    pieces,
    groups,
    depth_tile,
    feat_ref,
    weight_ref,
    grad_ref,
    *refs,
):
    n_chip = n_col // 2
    act_out, feat_out, slope_out, own_out = refs[:4]
    part_outs = refs[4 : 4 + n_chip - 1]
    (
        weight,
        feats,
        slopes,
        partial,
        partial_send,
        partial_recv,
        act,
        slopes_t,
        fgrad_t,
        fgrad,
        sib_send,
        sib_recv,
        own,
        parts,
        weight_sem,
        out_sem,
        part_sem,
        gather_send,
        gather_recv,
        forward_send,
        forward_recv,
        reduce_send,
        reduce_recv,
        slope_send,
        slope_recv,
        sib_send_sem,
        sib_recv_sem,
    ) = refs[4 + n_chip - 1 :]

    me_row = lax.axis_index("row")
    me_col = lax.axis_index("col")
    core = lax.rem(me_col, 2)
    chip = lax.div(me_col, 2)
    sibling = chip * 2 + (1 - core)
    mine = feat_ref.shape[0]
    kept = grad_ref.shape[0]
    depth, width = weight_ref.shape
    n_chunks = width // chunk

    def chip_at(step):
        return lax.rem(chip + step, n_chip)

    def chip_back(step):
        return lax.rem(chip + n_chip - step, n_chip)

    def row_at(step):
        return lax.rem(me_row + step, n_row)

    def cols(j):
        return pl.ds(j * chunk, chunk)

    piece = depth // pieces

    def span(p):
        return pl.ds(p * piece, piece)

    loads = []
    for j in range(n_chunks):
        load = pltpu.make_async_copy(
            weight_ref.at[:, cols(j)], weight.at[:, cols(j)], weight_sem.at[j]
        )
        load.start()
        loads.append(load)

    barrier = pltpu.get_barrier_semaphore()
    for step in range(1, n_chip):
        pl.semaphore_signal(
            barrier, inc=1, device_id=(me_row, chip_at(step) * 2 + core), device_id_type=MESH
        )
    pl.semaphore_signal(barrier, inc=1, device_id=(me_row, sibling), device_id_type=MESH)
    for step in range(1, n_row):
        pl.semaphore_signal(barrier, inc=1, device_id=(row_at(step), me_col), device_id_type=MESH)
    pl.semaphore_wait(barrier, n_chip + n_row - 1)

    sends = []
    gathers = []
    for step in range(1, n_chip):
        copy = pltpu.make_async_remote_copy(
            src_ref=feat_ref,
            dst_ref=feats.at[rows_at(me_col, mine)],
            send_sem=gather_send.at[step],
            recv_sem=gather_recv.at[step],
            device_id=(me_row, chip_at(step) * 2 + core),
            device_id_type=MESH,
        )
        copy.start()
        gathers.append(copy)
        sends.append(copy)
    forwards = []
    for step in range(n_chip):
        block = rows_at(chip_back(step) * 2 + core, mine)
        if step > 0:
            gathers[step - 1].wait_recv()
        copy = pltpu.make_async_remote_copy(
            src_ref=feat_ref if step == 0 else feats.at[block],
            dst_ref=feats.at[block],
            send_sem=forward_send.at[step],
            recv_sem=forward_recv.at[step],
            device_id=(me_row, sibling),
            device_id_type=MESH,
        )
        copy.start()
        forwards.append(copy)
        sends.append(copy)
        if step == 0:
            feats[rows_at(me_col, mine), :] = feat_ref[...]
    for copy in forwards:
        copy.wait_recv()
    outs = [pltpu.make_async_copy(feats, feat_out, out_sem.at[0])]
    outs[0].start()

    reduces = {}
    spreads = {}

    def multiply(j):
        loads[j].wait()
        total = jnp.dot(feats[...], weight[:, cols(j)], preferred_element_type=F32)
        partial[:, cols(j)] = total
        partial_send[:, cols(j)] = total.astype(BF16)
        reduces[j] = []
        for step in range(1, n_row):
            copy = pltpu.make_async_remote_copy(
                src_ref=partial_send.at[rows_at(row_at(step), kept), cols(j)],
                dst_ref=partial_recv.at[step - 1, :, cols(j)],
                send_sem=reduce_send.at[step - 1, j],
                recv_sem=reduce_recv.at[step - 1, j],
                device_id=(row_at(step), me_col),
                device_id_type=MESH,
            )
            copy.start()
            reduces[j].append(copy)
            sends.append(copy)

    def activate(j):
        for copy in reduces[j]:
            copy.wait_recv()
        preact = partial[rows_at(me_row, kept), cols(j)]
        for step in range(1, n_row):
            preact = preact + partial_recv[step - 1, :, cols(j)].astype(F32)
        sig = 1.0 / (1.0 + jnp.exp(-preact))
        slope = grad_ref[:, cols(j)].astype(F32) * silu_slope(preact, sig)
        slopes[rows_at(me_row, kept), cols(j)] = slope.astype(BF16)
        spreads[j] = []
        for step in range(1, n_row):
            block = slopes.at[rows_at(me_row, kept), cols(j)]
            copy = pltpu.make_async_remote_copy(
                src_ref=block,
                dst_ref=block,
                send_sem=slope_send.at[step - 1, j],
                recv_sem=slope_recv.at[step - 1, j],
                device_id=(row_at(step), me_col),
                device_id_type=MESH,
            )
            copy.start()
            spreads[j].append(copy)
            sends.append(copy)
        act[:, cols(j)] = (preact * sig).astype(BF16)

    def arrive(g):
        first, last = groups[g]
        for j in range(first, last):
            for copy in spreads[j]:
                copy.wait_recv()
            slopes_t[cols(j), :] = slopes[:, cols(j)].T

    def back(g, part, n_parts):
        first, last = groups[g]
        units = pl.ds(first * chunk, (last - first) * chunk)
        base = part * (depth // n_parts)

        @pl.loop(0, depth // n_parts // depth_tile)
        def _(t):
            at = pl.ds(pl.multiple_of(base + t * depth_tile, depth_tile), depth_tile)
            total = jnp.dot(weight[at, units], slopes_t[units, :], preferred_element_type=F32)
            if g > 0:
                total = total + fgrad_t[at, :]
            if g < len(groups) - 1:
                fgrad_t[at, :] = total
            else:
                fgrad[:, at] = total.T

    for j in range(n_chunks):
        multiply(j)
        if j >= 2:
            activate(j - 2)
    if n_chunks > 1:
        activate(n_chunks - 2)
    if len(groups) > 1:
        arrive(0)
        back(0, 0, 2)
    activate(n_chunks - 1)
    outs.append(pltpu.make_async_copy(act, act_out, out_sem.at[1]))
    outs[-1].start()
    if len(groups) > 1:
        back(0, 1, 2)
    for g in range(1, len(groups) - 1):
        arrive(g)
        back(g, 0, 1)
    arrive(len(groups) - 1)
    outs.append(pltpu.make_async_copy(slopes, slope_out, out_sem.at[2]))
    outs[-1].start()

    swaps = []
    for p in range(pieces):
        back(len(groups) - 1, p, pieces)
        for step in range(n_chip):
            theirs = chip_at(step) * 2 + (1 - core)
            sib_send[step, :, span(p)] = fgrad[rows_at(theirs, mine), span(p)].astype(BF16)
        copy = pltpu.make_async_remote_copy(
            src_ref=sib_send.at[:, :, span(p)],
            dst_ref=sib_recv.at[:, :, span(p)],
            send_sem=sib_send_sem.at[p],
            recv_sem=sib_recv_sem.at[p],
            device_id=(me_row, sibling),
            device_id_type=MESH,
        )
        copy.start()
        swaps.append(copy)
        sends.append(copy)
    for p in range(pieces):
        swaps[p].wait_recv()
        for step in range(n_chip):
            held = fgrad[rows_at(chip_at(step) * 2 + core, mine), span(p)]
            total = held + sib_recv[step, :, span(p)].astype(F32)
            if step == 0:
                own[:, span(p)] = total
            else:
                parts[step - 1, :, span(p)] = total.astype(BF16)
    for step in range(1, n_chip):
        outs.append(
            pltpu.make_async_copy(parts.at[step - 1], part_outs[step - 1], part_sem.at[step - 1])
        )
        outs[-1].start()
    outs.append(pltpu.make_async_copy(own, own_out, out_sem.at[3]))
    outs[-1].start()
    for copy in sends:
        copy.wait_send()
    for copy in outs:
        copy.wait()


def exchange(mesh, features, weight, act_grad):
    n_row, n_col = mesh.shape["row"], mesh.shape["col"]
    n_chip = n_col // 2
    mine, depth = features.shape
    kept, width = act_grad.shape
    examples = mine * n_col
    chunk = width // 8 if width >= 4096 else width
    n_chunks = width // chunk
    pieces = 4 if depth >= 4096 else 1
    groups = ((0, 4), (4, 7), (7, 8)) if n_chunks == 8 else ((0, n_chunks),)
    depth_tile = min(1024, depth)
    anywhere = pl.BlockSpec(memory_space=pl.ANY)
    vmem = pl.BlockSpec(memory_space=pltpu.VMEM)
    flops = 4 * examples * depth * width
    dma = pltpu.SemaphoreType.DMA
    return pl.pallas_call(
        functools.partial(exchange_kernel, n_row, n_col, chunk, pieces, groups, depth_tile),
        out_shape=[
            jax.ShapeDtypeStruct((kept, width), BF16),
            jax.ShapeDtypeStruct((examples, depth), BF16),
            jax.ShapeDtypeStruct((examples, width), BF16),
            jax.ShapeDtypeStruct((mine, depth), F32),
        ]
        + [jax.ShapeDtypeStruct((mine, depth), BF16)] * (n_chip - 1),
        in_specs=[vmem, anywhere, vmem],
        out_specs=[anywhere] * (4 + n_chip - 1),
        scratch_shapes=[
            pltpu.VMEM((depth, width), BF16),
            pltpu.VMEM((examples, depth), BF16),
            pltpu.VMEM((examples, width), BF16),
            pltpu.VMEM((examples, width), F32),
            pltpu.VMEM((examples, width), BF16),
            pltpu.VMEM((n_row - 1, kept, width), BF16),
            pltpu.VMEM((kept, width), BF16),
            pltpu.VMEM((width, examples), BF16),
            pltpu.VMEM((depth, examples), F32),
            pltpu.VMEM((examples, depth), F32),
            pltpu.VMEM((n_chip, mine, depth), BF16),
            pltpu.VMEM((n_chip, mine, depth), BF16),
            pltpu.VMEM((mine, depth), F32),
            pltpu.VMEM((n_chip - 1, mine, depth), BF16),
            dma((n_chunks,)),
            dma((4,)),
            dma((n_chip - 1,)),
            dma((n_chip,)),
            dma((n_chip,)),
            dma((n_chip,)),
            dma((n_chip,)),
            dma((n_row - 1, n_chunks)),
            dma((n_row - 1, n_chunks)),
            dma((n_row - 1, n_chunks)),
            dma((n_row - 1, n_chunks)),
            dma((pieces,)),
            dma((pieces,)),
        ],
        compiler_params=pltpu.CompilerParams(
            collective_id=0, has_side_effects=True, vmem_limit_bytes=56 * 1024 * 1024
        ),
        cost_estimate=pl.CostEstimate(
            flops=flops, bytes_accessed=2 * depth * width, transcendentals=kept * width
        ),
    )(features, weight, act_grad)


def outer_kernel(feat_ref, slope_ref, out_ref):
    out_ref[...] = lax.dot_general(
        feat_ref[...], slope_ref[...], (((0,), (0,)), ((), ())), preferred_element_type=F32
    )


def outer(features, slopes):
    examples, depth = features.shape
    width = slopes.shape[1]
    tall, wide = min(1024, depth), min(1024, width)
    return pl.pallas_call(
        outer_kernel,
        grid=(depth // tall, width // wide),
        out_shape=jax.ShapeDtypeStruct((depth, width), F32),
        in_specs=[
            pl.BlockSpec((examples, tall), lambda i, j: (0, i)),
            pl.BlockSpec((examples, wide), lambda i, j: (0, j)),
        ],
        out_specs=pl.BlockSpec((tall, wide), lambda i, j: (i, j)),
        compiler_params=pltpu.CompilerParams(vmem_limit_bytes=60 * 1024 * 1024),
        cost_estimate=pl.CostEstimate(
            flops=2 * examples * depth * width,
            bytes_accessed=4 * depth * width,
            transcendentals=0,
        ),
    )(features, slopes)


def shards(mesh, embeddings, projection, weight, act_grad):
    n_chip = mesh.shape["col"] // 2
    emb_rows = weight.shape[0] // projection.shape[1]
    emb_first = lax.axis_index("row") * emb_rows
    mine_emb = lax.dynamic_slice_in_dim(embeddings, emb_first, emb_rows, 1)
    gram = jnp.einsum(
        "bid,bmd->bim", mine_emb, embeddings, preferred_element_type=F32
    ).astype(BF16)
    features = jnp.einsum("bim,mr->bir", gram, projection, preferred_element_type=F32)
    features = features.astype(BF16).reshape(embeddings.shape[0], -1)
    activation, features_all, slopes_all, own, *parts = exchange(
        mesh, features, weight, act_grad
    )
    arrived = []
    for step in range(1, n_chip):
        pairs = [
            (2 * z + core, 2 * ((z + step) % n_chip) + core)
            for z in range(n_chip)
            for core in range(2)
        ]
        arrived.append(lax.ppermute(parts[step - 1], "col", pairs))
    weight_grad = outer(features_all, slopes_all)
    feature_grad = own
    for block in arrived:
        feature_grad = feature_grad + block.astype(F32)
    return activation, weight_grad, feature_grad


def solution(mesh):
    return jax.shard_map(
        functools.partial(shards, mesh),
        mesh=mesh,
        in_specs=(P("col", None, None), P(), P("row", "col"), P("row", "col")),
        out_specs=(P("row", "col"), P("row", "col"), P("col", "row")),
        check_vma=False,
    )
```
